32 devices in a mesh: section: 2 (over core), dom: 16 (over z, y, x).
Axes of the slice: x: 2, y: 2, z: 4, core: 2. Of those that a mesh axis runs over, the one named last changes fastest.
Arguments:
- node_feats: bfloat16 [2, 4096, 512], P(None, 'dom'), may hold values from -6 to 6
- edge_feats: bfloat16 [2, 8192, 512], P(None, 'dom'), may hold values from -6 to 6
- edge_src: int32 [8192], P('dom'), may hold values from 0 to 287, as said below
- edge_dst: int32 [8192], P('dom'), may hold values from 0 to 255
- edge_count: int32 [16], P('dom'), may hold values from 256 to 512, as said below
- send_rows: int32 [256, 2], P('dom'), may hold values from 0 to 255
- edge_w1: bfloat16 [2, 3, 512, 512], P('section'), may hold values from -0.15625 to 0.15625
- edge_b1: bfloat16 [2, 512], P('section'), may hold values from -3 to 3
- edge_w2: bfloat16 [2, 512, 512], P('section'), may hold values from -0.25 to 0.25
- edge_gain: bfloat16 [2, 512], P('section'), may hold values from 0.5 to 1.5
- node_w1: bfloat16 [2, 2, 512, 512], P('section'), may hold values from -0.1875 to 0.1875
- node_b1: bfloat16 [2, 512], P('section'), may hold values from -3 to 3
- node_w2: bfloat16 [2, 512, 512], P('section'), may hold values from -0.25 to 0.25
- node_gain: bfloat16 [2, 512], P('section'), may hold values from 0.5 to 1.5
Outputs:
- node_out: bfloat16 [2, 2, 4096, 512], P('section', None, 'dom')
- edge_out: bfloat16 [2, 2, 8192, 512], P('section', None, 'dom')
The draws below stay inside these ranges and needn't reach their ends.
Inputs may be any that keep to these rules, and one draw needn't show every extreme that they name: `edge_src`: among a device's 512 slots, the first 32 name each value from 256 upward exactly once; the others are below 256. `edge_count`: some device has all 512 slots live.
All inputs are finite; a program needn't handle non-finite values.
Results may differ from the reference program's by a relative error of at most 0.0065.
Values may be sent and summed in bfloat16 or wider, within the bound.
A program may use at most 64 MiB of HBM per device.

```python
import jax
import jax.numpy as jnp
from jax import lax

D = 512
H = 512
NODE_DEV = 256
EDGE_DEV = 512
HCAP = 2
MB = 2
LAYERS = 2
PEERS = 16
NODES = 4096
EDGES = 8192


def draw_edge_src(key, part):
    key_list = jax.random.split(key, PEERS)
    halo_slots = jax.vmap(lambda single: jax.random.permutation(single, PEERS * HCAP))(key_list) + NODE_DEV
    local_rows = jax.random.randint(jax.random.fold_in(key, 7), (PEERS, EDGE_DEV - PEERS * HCAP), 0, NODE_DEV)
    return jnp.concatenate([halo_slots.astype(jnp.int32), local_rows.astype(jnp.int32)], axis=1).reshape(-1)


def draw_edge_count(key, part):
    counts = jax.random.randint(key, (PEERS,), EDGE_DEV // 2, EDGE_DEV + 1)
    fullest = jax.random.randint(jax.random.fold_in(key, 11), (), 0, PEERS)
    return counts.at[fullest].set(EDGE_DEV).astype(jnp.int32)


def plant(result, key, smallest, largest):
    longest = result.shape.index(max(result.shape))
    spots = []
    for shift in (0, 1):
        where = [jax.random.randint(jax.random.fold_in(key, axis), (), 0, length) for axis, length in enumerate(result.shape)]
        where[longest] = (where[longest] + shift) % result.shape[longest]
        spots.append(tuple(where))
    return result.at[spots[0]].set(smallest).at[spots[1]].set(largest)


def block_scale(key, shape, pieces, least, top_value):
    loudness, own = 1.0, jax.random.fold_in(key, 6)
    for axis_at, parts in pieces:
        draws = jnp.exp(jax.random.uniform(jax.random.fold_in(own, axis_at), (parts,), jnp.float32, least / len(pieces), top_value / len(pieces)))
        loudness = loudness * jnp.repeat(draws, shape[axis_at] // parts).reshape([-1 if axis == axis_at else 1 for axis in range(len(shape))])
    return loudness


def gaussian(rng, extent, deviation, bound, cuts=(), kind=jnp.bfloat16):
    result = jax.random.normal(rng, extent, jnp.float32) * deviation
    if len(cuts) > 0:
        result = block_scale(rng, extent, cuts, -0.22, 0.18) * result
    return jnp.clip(result, min=-bound, max=bound).astype(kind)


def setup_inputs(seed: int = 0) -> dict:
    splits = jax.random.split(jax.random.key(seed), 15)
    node_feats = gaussian(splits[0], (MB, NODES, D), 1.0, 6.0, ((1, 16),))
    edge_feats = gaussian(splits[1], (MB, EDGES, D), 1.0, 6.0, ((1, 16),))
    edge_src = draw_edge_src(jax.random.fold_in(splits[14], 71), 0)
    edge_dst = plant(jax.random.randint(splits[3], (EDGES,), 0, NODE_DEV), jax.random.fold_in(splits[3], 1), 0, NODE_DEV - 1).astype(jnp.int32)
    edge_count = draw_edge_count(jax.random.fold_in(splits[14], 71), 0)
    send_rows = plant(jax.random.randint(splits[5], (PEERS * PEERS, HCAP), 0, NODE_DEV), jax.random.fold_in(splits[5], 1), 0, NODE_DEV - 1).astype(jnp.int32)
    edge_w1 = gaussian(splits[6], (LAYERS, 3, D, H), (3 * D) ** -0.5, 0.15625, ((0, 2),))
    edge_b1 = gaussian(splits[7], (LAYERS, H), 0.5, 3.0, ((0, 2),))
    edge_w2 = gaussian(splits[8], (LAYERS, H, D), H ** -0.5, 0.25, ((0, 2),))
    edge_gain = jnp.clip(1.0 + 0.1 * jax.random.normal(splits[9], (LAYERS, D), jnp.float32), 0.5, 1.5).astype(jnp.bfloat16)
    node_w1 = gaussian(splits[10], (LAYERS, 2, D, H), (2 * D) ** -0.5, 0.1875, ((0, 2),))
    node_b1 = gaussian(splits[11], (LAYERS, H), 0.5, 3.0, ((0, 2),))
    node_w2 = gaussian(splits[12], (LAYERS, H, D), H ** -0.5, 0.25, ((0, 2),))
    node_gain = jnp.clip(1.0 + 0.1 * jax.random.normal(splits[13], (LAYERS, D), jnp.float32), 0.5, 1.5).astype(jnp.bfloat16)
    return dict(node_feats=node_feats, edge_feats=edge_feats, edge_src=edge_src, edge_dst=edge_dst, edge_count=edge_count, send_rows=send_rows, edge_w1=edge_w1, edge_b1=edge_b1, edge_w2=edge_w2, edge_gain=edge_gain, node_w1=node_w1, node_b1=node_b1, node_w2=node_w2, node_gain=node_gain)


def layer_norm(values, gain):
    row_mean = lax.optimization_barrier(jnp.mean(values, axis=-1, keepdims=True))
    centred = values - row_mean
    row_var = lax.optimization_barrier(jnp.mean(centred * centred, axis=-1, keepdims=True))
    return centred * lax.rsqrt(row_var + 1e-05) * gain.astype(jnp.float32)

def apply_layer(node_lat, edge_lat, weights, sender, receiver, live_mask):
    edge_w1, edge_b1, edge_w2, edge_gain, node_w1, node_b1, node_w2, node_gain = weights
    from_sender = jnp.dot(node_lat, edge_w1[1], preferred_element_type=jnp.float32)
    from_receiver = jnp.dot(node_lat, edge_w1[2], preferred_element_type=jnp.float32)

    def one_device(items):
        block_edges, block_sender, block_receiver, block_live = items
        hidden = jnp.dot(block_edges, edge_w1[0], preferred_element_type=jnp.float32)
        hidden = hidden + from_sender[block_sender] + from_receiver[block_receiver] + edge_b1.astype(jnp.float32)
        hidden = jax.nn.silu(hidden).astype(jnp.bfloat16)
        update = layer_norm(jnp.dot(hidden, edge_w2, preferred_element_type=jnp.float32), edge_gain)
        update = update * block_live[:, None]
        new_edges = (block_edges.astype(jnp.float32) + update).astype(jnp.bfloat16)
        return (new_edges, update.astype(jnp.bfloat16))
    new_edges, message = lax.map(one_device, (edge_lat.reshape(PEERS, EDGE_DEV, D), sender, receiver, live_mask))
    incoming = jax.ops.segment_sum(message.reshape(-1, D).astype(jnp.float32), receiver.reshape(-1), num_segments=NODES)
    incoming = incoming.astype(jnp.bfloat16)
    node_hidden = jnp.dot(node_lat, node_w1[0], preferred_element_type=jnp.float32)
    node_hidden = node_hidden + jnp.dot(incoming, node_w1[1], preferred_element_type=jnp.float32) + node_b1.astype(jnp.float32)
    node_hidden = jax.nn.silu(node_hidden).astype(jnp.bfloat16)
    node_update = layer_norm(jnp.dot(node_hidden, node_w2, preferred_element_type=jnp.float32), node_gain)
    new_nodes = (node_lat.astype(jnp.float32) + node_update).astype(jnp.bfloat16)
    return (new_nodes, new_edges.reshape(-1, D))

def reference(node_feats, edge_feats, edge_src, edge_dst, edge_count, send_rows, edge_w1, edge_b1, edge_w2, edge_gain, node_w1, node_b1, node_w2, node_gain):
    source = edge_src.reshape(PEERS, EDGE_DEV)
    target = edge_dst.reshape(PEERS, EDGE_DEV)
    owner_dev = jnp.arange(PEERS, dtype=jnp.int32)[:, None]
    halo_slot = jnp.clip(source - NODE_DEV, 0, PEERS * HCAP - 1).astype(jnp.int32)
    peer_dev = halo_slot // HCAP
    slot_part = halo_slot % HCAP
    remote = peer_dev * NODE_DEV + send_rows[peer_dev * PEERS + owner_dev, slot_part]
    sender = jnp.where(source < NODE_DEV, owner_dev * NODE_DEV + source, remote).astype(jnp.int32)
    receiver = (owner_dev * NODE_DEV + target).astype(jnp.int32)
    positions = jnp.arange(EDGE_DEV, dtype=jnp.int32)[None, :]
    live_mask = (positions < edge_count[:, None]).astype(jnp.float32)
    node_layers = []
    edge_layers = []
    current_nodes = [node_feats[batch_num] for batch_num in range(MB)]
    current_edges = [edge_feats[batch_num] for batch_num in range(MB)]
    for layer_num in range(LAYERS):
        weights = (edge_w1[layer_num], edge_b1[layer_num], edge_w2[layer_num], edge_gain[layer_num], node_w1[layer_num], node_b1[layer_num], node_w2[layer_num], node_gain[layer_num])
        for batch_num in range(MB):
            current_nodes[batch_num], current_edges[batch_num] = apply_layer(current_nodes[batch_num], current_edges[batch_num], weights, sender, receiver, live_mask)
        node_layers.append(jnp.stack(current_nodes))
        edge_layers.append(jnp.stack(current_edges))
    return (jnp.stack(node_layers), jnp.stack(edge_layers))
```

```python
import functools

import jax
import jax.numpy as jnp
from jax import lax
from jax.experimental import pallas as pl
from jax.experimental.pallas import tpu as pltpu
from jax.sharding import PartitionSpec as P

F32 = jnp.float32
BF16 = jnp.bfloat16
LANES = 128
BLOCK = 256


def dot(lhs, rhs):
    return jnp.dot(lhs, rhs, preferred_element_type=F32)


def silu(x):
    half = 0.5 * x
    return half + half * jnp.tanh(half)


def layer_norm(values, gain):
    row_mean = jnp.mean(values, axis=-1, keepdims=True)
    centred = values - row_mean
    row_var = jnp.mean(centred * centred, axis=-1, keepdims=True)
    return centred * lax.rsqrt(row_var + 1e-05) * gain


def column(row):
    return jnp.broadcast_to(row, (LANES, row.shape[1])).T


def onehot(col, width):
    parts = []
    for start in range(0, width, LANES):
        size = min(LANES, width - start)
        lane = lax.broadcasted_iota(jnp.int32, (col.shape[0], size), 1) + start
        parts.append((col[:, :size] == lane).astype(F32).astype(BF16))
    return parts[0] if len(parts) == 1 else jnp.concatenate(parts, axis=1)


def kernel(peers, hcap, chunks,
           cnt, src, dst, send, eb1, eg, nb1, ng,
           nf, ef, ew1, ew2, nw1, nw2,
           no, eo,
           nl, el, onl, oel, rhs, w1r, w2, n1, n2, msg, ohs, ohr, ohrt,
           out0, out1, halo, hx,
           wsem, lsem, hsem, osem, s0sem, s1sem, ssem):
    batches, nodes, width = nl.shape
    edges = el.shape[1]
    halo_rows = peers * hcap
    sec = lax.axis_index("section")
    me = lax.axis_index("dom")
    barrier = pltpu.get_barrier_semaphore()

    def hail(section, target):
        pl.semaphore_signal(barrier, inc=1, device_id={"section": section, "dom": target},
                            device_id_type=pl.DeviceIdType.MESH)

    def peer(step):
        return lax.rem(me + step, peers)

    @pl.loop(0, peers)
    def _(step):
        hail(1 - sec, peer(step))

    @pl.when(sec == 0)
    def _():
        @pl.loop(1, peers)
        def _(step):
            hail(0, peer(step))

    at_e, at_r, at_s = nodes, nodes + width, 2 * nodes + width

    def load(index, source, target):
        return pltpu.make_async_copy(source, target, wsem.at[index])

    weights = [
        load(0, ew1.at[0, 1], rhs.at[pl.ds(at_s, width)]),
        load(1, ew1.at[0, 2], w1r),
        load(2, ew1.at[0, 0], rhs.at[pl.ds(at_e, width)]),
        load(3, ew2.at[0], w2),
        load(4, nw1.at[0, 0], n1.at[pl.ds(0, width)]),
        load(5, nw1.at[0, 1], n1.at[pl.ds(width, width)]),
        load(6, nw2.at[0], n2),
    ]

    def node_in(m):
        return pltpu.make_async_copy(nf.at[m], nl.at[m], lsem.at[m, 0])

    def edge_in(m, c):
        lo, hi = chunks[c]
        return pltpu.make_async_copy(ef.at[m, pl.ds(lo, hi - lo)], el.at[m, pl.ds(lo, hi - lo)],
                                     lsem.at[m, 1 + c])

    @pl.when(sec == 0)
    def _():
        for m in range(batches):
            node_in(m).start()

    for copy in weights[:3]:
        copy.start()

    @pl.when(sec == 0)
    def _():
        for c in range(len(chunks)):
            edge_in(0, c).start()

    for copy in weights[3:]:
        copy.start()

    @pl.when(sec == 0)
    def _():
        for m in range(1, batches):
            for c in range(len(chunks)):
                edge_in(m, c).start()

    send_hot = jnp.concatenate(
        [(lax.broadcasted_iota(jnp.int32, (peers, nodes), 1) == send[:, k:k + 1]).astype(F32)
         for k in range(hcap)], axis=0).astype(BF16)

    def gather_rows(values, store):
        rows = dot(send_hot, values)
        for t in range(peers):
            for k in range(hcap):
                store(t, k, rows[k * peers + t:k * peers + t + 1])

    @pl.when(sec == 0)
    def _():
        for m in range(batches):
            node_in(m).wait()

            def store(t, k, row, m=m):
                out0[t, m, pl.ds(k, 1)] = row

            gather_rows(nl[m], store)
        pl.semaphore_wait(barrier, 2 * peers - 1)

        @pl.loop(1, peers)
        def _(step):
            target = peer(step)
            pltpu.make_async_remote_copy(
                src_ref=out0.at[target], dst_ref=halo.at[me], send_sem=s0sem, recv_sem=hsem.at[0],
                device_id={"section": 0, "dom": target}, device_id_type=pl.DeviceIdType.MESH).start()

        pltpu.make_async_copy(out0.at[me], halo.at[me], hsem.at[0]).start()

    @pl.when(sec == 1)
    def _():
        pl.semaphore_wait(barrier, peers)

    col_s = column(src[...])
    col_r = column(dst[...])
    ohs[...] = onehot(col_s, nodes)
    ohr[...] = onehot(col_r, nodes)
    ohrt[...] = (lax.broadcasted_iota(jnp.int32, (nodes, edges), 0) == dst[...]).astype(F32).astype(BF16)
    halo_hot = onehot(col_s[:halo_rows] - nodes, halo_rows)

    bias_e = eb1[...].astype(F32)
    gain_e = eg[...].astype(F32)
    bias_n = nb1[...].astype(F32)
    gain_n = ng[...].astype(F32)
    live = cnt[0]

    def to_next(m, slot, source, target):
        return pltpu.make_async_remote_copy(
            src_ref=source, dst_ref=target, send_sem=ssem.at[m, slot], recv_sem=lsem.at[m, slot],
            device_id={"section": 1, "dom": me}, device_id_type=pl.DeviceIdType.MESH)

    def node_next(m):
        return to_next(m, 0, onl.at[m], nl.at[m])

    def edge_next(m, c):
        lo, hi = chunks[c]
        rows = pl.ds(lo, hi - lo)
        return to_next(m, 1 + c, oel.at[m, rows], el.at[m, rows])

    def node_res(m):
        return pltpu.make_async_copy(onl.at[m], no.at[0, m], osem.at[m, 0])

    def edge_res(m, c):
        lo, hi = chunks[c]
        rows = pl.ds(lo, hi - lo)
        return pltpu.make_async_copy(oel.at[m, rows], eo.at[0, m, rows], osem.at[m, 1 + c])

    for m in range(batches):
        @pl.when(sec == 1)
        def _():
            node_in(m).wait()

        if m == 0:
            weights[0].wait()
            weights[1].wait()
        values = nl[m]
        rhs[:nodes] = dot(values, rhs[at_s:]).astype(BF16)
        rhs[at_r:at_s] = dot(values, w1r[...]).astype(BF16)

        for c in list(range(1, len(chunks))) + [0]:
            lo, hi = chunks[c]
            edge_in(m, c).wait()
            if m == 0 and c == 1:
                weights[2].wait()
                weights[3].wait()
            if c == 0:
                if m == 0:
                    @pl.when(sec == 0)
                    def _():
                        pltpu.make_async_copy(halo, halo, hsem.at[0]).wait()

                @pl.when(sec == 1)
                def _():
                    pltpu.make_async_copy(halo.at[:, m], halo.at[:, m], hsem.at[m]).wait()

                for p in range(peers):
                    hx[pl.ds(p * hcap, hcap)] = halo[p, m]
                from_far = dot(halo_hot, hx[...].astype(BF16)).astype(BF16)
                lat = el[m, lo:hi]
                lhs = jnp.concatenate([lat, ohr[lo:hi], from_far], axis=1)
                pre = dot(lhs, rhs[at_e:])
            else:
                lat = el[m, lo:hi]
                lhs = jnp.concatenate([ohs[lo:hi], lat, ohr[lo:hi]], axis=1)
                pre = dot(lhs, rhs[:at_s])
            hidden = silu(pre + bias_e).astype(BF16)
            update = layer_norm(dot(hidden, w2[...]), gain_e)
            slot = lax.broadcasted_iota(jnp.int32, (hi - lo, 1), 0) + lo
            update = update * (slot < live).astype(F32)
            msg[lo:hi] = update.astype(BF16)
            oel[m, lo:hi] = (lat.astype(F32) + update).astype(BF16)

            @pl.when(sec == 0)
            def _():
                edge_next(m, c).start()

            edge_res(m, c).start()

        if m == 0:
            for copy in weights[4:]:
                copy.wait()
        incoming = dot(ohrt[...], msg[...]).astype(BF16)
        values = nl[m]
        pre = dot(jnp.concatenate([values, incoming], axis=1), n1[...])
        hidden = silu(pre + bias_n).astype(BF16)
        update = layer_norm(dot(hidden, n2[...]), gain_n)
        onl[m] = (values.astype(F32) + update).astype(BF16)

        @pl.when(sec == 0)
        def _():
            node_next(m).start()

            def store(t, k, row):
                out1[m, t, pl.ds(k, 1)] = row

            gather_rows(onl[m], store)

            @pl.loop(0, peers)
            def _(step):
                target = peer(step)
                pltpu.make_async_remote_copy(
                    src_ref=out1.at[m, target], dst_ref=halo.at[me, m], send_sem=s1sem.at[m],
                    recv_sem=hsem.at[m], device_id={"section": 1, "dom": target},
                    device_id_type=pl.DeviceIdType.MESH).start()

        node_res(m).start()

    for m in range(batches):
        node_res(m).wait()
        for c in range(len(chunks)):
            edge_res(m, c).wait()

    @pl.when(sec == 0)
    def _():
        others = out0.at[pl.ds(0, peers - 1)]
        pltpu.make_async_copy(others, others, s0sem).wait()
        for m in range(batches):
            pltpu.make_async_copy(out1.at[m], out1.at[m], s1sem.at[m]).wait()
            node_next(m).wait_send()
            for c in range(len(chunks)):
                edge_next(m, c).wait_send()


def local(node_feats, edge_feats, edge_src, edge_dst, edge_count, send_rows,
          edge_w1, edge_b1, edge_w2, edge_gain, node_w1, node_b1, node_w2, node_gain):
    batches, nodes, width = node_feats.shape
    edges = edge_feats.shape[1]
    peers, hcap = send_rows.shape
    inner = edge_w2.shape[1]
    halo_rows = peers * hcap
    chunks = [(0, halo_rows)]
    while chunks[-1][1] < edges:
        start = chunks[-1][1]
        chunks.append((start, min(edges, (start // BLOCK + 1) * BLOCK)))
    slots = len(chunks) + 1
    anywhere = pl.BlockSpec(memory_space=pl.ANY)
    vmem = pl.BlockSpec(memory_space=pltpu.VMEM)
    dma = pltpu.SemaphoreType.DMA
    flops = 2 * batches * width * inner * (3 * edges + 6 * nodes)
    moved = 2 * (2 * batches * (nodes + edges) * width + 7 * width * inner)
    return pl.pallas_call(
        functools.partial(kernel, peers, hcap, chunks),
        out_shape=(jax.ShapeDtypeStruct((1, batches, nodes, width), BF16),
                   jax.ShapeDtypeStruct((1, batches, edges, width), BF16)),
        in_specs=[pl.BlockSpec(memory_space=pltpu.SMEM)] + [vmem] * 7 + [anywhere] * 6,
        out_specs=(anywhere, anywhere),
        scratch_shapes=[
            pltpu.VMEM((batches, nodes, width), BF16),
            pltpu.VMEM((batches, edges, width), BF16),
            pltpu.VMEM((batches, nodes, width), BF16),
            pltpu.VMEM((batches, edges, width), BF16),
            pltpu.VMEM((2 * nodes + 2 * width, inner), BF16),
            pltpu.VMEM((width, inner), BF16),
            pltpu.VMEM((inner, width), BF16),
            pltpu.VMEM((2 * width, inner), BF16),
            pltpu.VMEM((inner, width), BF16),
            pltpu.VMEM((edges, width), BF16),
            pltpu.VMEM((edges, nodes), BF16),
            pltpu.VMEM((edges, nodes), BF16),
            pltpu.VMEM((nodes, edges), BF16),
            pltpu.VMEM((peers, batches, hcap, width), F32),
            pltpu.VMEM((batches, peers, hcap, width), F32),
            pltpu.VMEM((peers, batches, hcap, width), F32),
            pltpu.VMEM((halo_rows, width), F32),
            dma((7,)),
            dma((batches, slots)),
            dma((batches,)),
            dma((batches, slots)),
            dma,
            dma((batches,)),
            dma((batches, slots)),
        ],
        compiler_params=pltpu.CompilerParams(
            collective_id=0, has_side_effects=True, vmem_limit_bytes=48 * 1024 * 1024),
        cost_estimate=pl.CostEstimate(flops=flops, bytes_accessed=moved, transcendentals=0),
    )(edge_count, edge_src.reshape(1, -1), edge_dst.reshape(1, -1), send_rows,
      edge_b1, edge_gain, node_b1, node_gain,
      node_feats, edge_feats, edge_w1, edge_w2, node_w1, node_w2)


def solution(mesh):
    in_specs = (
        P(None, "dom", None),
        P(None, "dom", None),
        P("dom"),
        P("dom"),
        P("dom"),
        P("dom", None),
        P("section", None, None, None),
        P("section", None),
        P("section", None, None),
        P("section", None),
        P("section", None, None, None),
        P("section", None),
        P("section", None, None),
        P("section", None),
    )
    out_specs = (P("section", None, "dom", None), P("section", None, "dom", None))
    return jax.shard_map(local, mesh=mesh, in_specs=in_specs, out_specs=out_specs, check_vma=False)
```

```python
import functools

import jax
import jax.numpy as jnp
from jax import lax
from jax.experimental import pallas as pl
from jax.experimental.pallas import tpu as pltpu
from jax.sharding import PartitionSpec as P

F32 = jnp.float32
BF16 = jnp.bfloat16
LANES = 128
BLOCK = 256


def dot(lhs, rhs):
    return jnp.dot(lhs, rhs, preferred_element_type=F32)


def silu(x):
    half = 0.5 * x
    return half + half * jnp.tanh(half)


def layer_norm(values, gain):
    row_mean = jnp.mean(values, axis=-1, keepdims=True)
    centred = values - row_mean
    row_var = jnp.mean(centred * centred, axis=-1, keepdims=True)
    return centred * lax.rsqrt(row_var + 1e-05) * gain


def column(row):
    return jnp.broadcast_to(row, (LANES, row.shape[1])).T


def onehot(col, width):
    parts = []
    for start in range(0, width, LANES):
        size = min(LANES, width - start)
        lane = lax.broadcasted_iota(jnp.int32, (col.shape[0], size), 1) + start
        parts.append((col[:, :size] == lane).astype(F32).astype(BF16))
    return parts[0] if len(parts) == 1 else jnp.concatenate(parts, axis=1)


def kernel(peers, hcap, chunks,
           cnt_in, src_in, dst_in, send_in, eb1_in, eg_in, nb1_in, ng_in,
           nf, ef, ew1, ew2, nw1, nw2,
           no, eo,
           cnt, src, dst, send, eb1, eg, nb1, ng, nl, el, onl, oel, rhs, w1r, w2, n1, n2, msg, ohs, ohr, ohrt,
           out0, out1, halo, hx,
           wsem, lsem, hsem, osem, s0sem, s1sem, ssem):
    batches, nodes, width = nl.shape
    edges = el.shape[1]
    halo_rows = peers * hcap
    sec = lax.axis_index("section")
    me = lax.axis_index("dom")
    barrier = pltpu.get_barrier_semaphore()

    def hail(section, target):
        pl.semaphore_signal(barrier, inc=1, device_id={"section": section, "dom": target},
                            device_id_type=pl.DeviceIdType.MESH)

    def peer(step):
        return lax.rem(me + step, peers)

    at_e, at_r, at_s = nodes, nodes + width, 2 * nodes + width

    def load(index, source, target):
        return pltpu.make_async_copy(source, target, wsem.at[index])

    weights = [
        load(0, ew1.at[0, 1], rhs.at[pl.ds(at_s, width)]),
        load(1, ew1.at[0, 2], w1r),
        load(2, ew1.at[0, 0], rhs.at[pl.ds(at_e, width)]),
        load(3, ew2.at[0], w2),
        load(4, nw1.at[0, 0], n1.at[pl.ds(0, width)]),
        load(5, nw1.at[0, 1], n1.at[pl.ds(width, width)]),
        load(6, nw2.at[0], n2),
    ]

    small = [load(7 + i, source, target) for i, (source, target) in enumerate([
        (send_in, send), (src_in, src), (dst_in, dst), (cnt_in, cnt),
        (eb1_in, eb1), (eg_in, eg), (nb1_in, nb1), (ng_in, ng)])]

    def node_in(m):
        return pltpu.make_async_copy(nf.at[m], nl.at[m], lsem.at[m, 0])

    def edge_in(m, c):
        lo, hi = chunks[c]
        return pltpu.make_async_copy(ef.at[m, pl.ds(lo, hi - lo)], el.at[m, pl.ds(lo, hi - lo)],
                                     lsem.at[m, 1 + c])

    small[0].start()

    @pl.when(sec == 0)
    def _():
        for m in range(batches):
            node_in(m).start()

    for copy in small[1:3] + weights[:3] + small[3:]:
        copy.start()

    @pl.loop(0, peers)
    def _(step):
        hail(1 - sec, peer(step))

    @pl.when(sec == 0)
    def _():
        @pl.loop(1, peers)
        def _(step):
            hail(0, peer(step))

    @pl.when(sec == 0)
    def _():
        for c in range(len(chunks)):
            edge_in(0, c).start()

    for copy in weights[3:]:
        copy.start()

    @pl.when(sec == 0)
    def _():
        for m in range(1, batches):
            for c in range(len(chunks)):
                edge_in(m, c).start()

    small[0].wait()
    send_hot = jnp.concatenate(
        [onehot(column(send[k:k + 1]), nodes) for k in range(hcap)], axis=0)

    def gather_rows(values, store):
        rows = dot(send_hot, values)
        for t in range(peers):
            for k in range(hcap):
                store(t, k, rows[k * peers + t:k * peers + t + 1])

    @pl.when(sec == 0)
    def _():
        for m in range(batches):
            node_in(m).wait()

            def store(t, k, row, m=m):
                out0[t, m, pl.ds(k, 1)] = row

            gather_rows(nl[m], store)
        pl.semaphore_wait(barrier, 2 * peers - 1)

        @pl.loop(1, peers)
        def _(step):
            target = peer(step)
            pltpu.make_async_remote_copy(
                src_ref=out0.at[target], dst_ref=halo.at[me], send_sem=s0sem, recv_sem=hsem.at[0],
                device_id={"section": 0, "dom": target}, device_id_type=pl.DeviceIdType.MESH).start()

        pltpu.make_async_copy(out0.at[me], halo.at[me], hsem.at[0]).start()

    @pl.when(sec == 1)
    def _():
        pl.semaphore_wait(barrier, peers)

    for copy in small[1:]:
        copy.wait()
    col_s = column(src[...])
    col_r = column(dst[...])
    ohs[...] = onehot(col_s, nodes)
    ohr[...] = onehot(col_r, nodes)
    ohrt[...] = (lax.broadcasted_iota(jnp.int32, (nodes, edges), 0) == dst[...]).astype(F32).astype(BF16)
    halo_hot = onehot(col_s[:halo_rows] - nodes, halo_rows)

    bias_e = eb1[...].astype(F32)
    gain_e = eg[...].astype(F32)
    bias_n = nb1[...].astype(F32)
    gain_n = ng[...].astype(F32)
    live = cnt[...]

    def to_next(m, slot, source, target):
        return pltpu.make_async_remote_copy(
            src_ref=source, dst_ref=target, send_sem=ssem.at[m, slot], recv_sem=lsem.at[m, slot],
            device_id={"section": 1, "dom": me}, device_id_type=pl.DeviceIdType.MESH)

    def node_next(m):
        return to_next(m, 0, onl.at[m], nl.at[m])

    def edge_next(m, c):
        lo, hi = chunks[c]
        rows = pl.ds(lo, hi - lo)
        return to_next(m, 1 + c, oel.at[m, rows], el.at[m, rows])

    def node_res(m):
        return pltpu.make_async_copy(onl.at[m], no.at[0, m], osem.at[m, 0])

    def edge_res(m, c):
        lo, hi = chunks[c]
        rows = pl.ds(lo, hi - lo)
        return pltpu.make_async_copy(oel.at[m, rows], eo.at[0, m, rows], osem.at[m, 1 + c])

    for m in range(batches):
        @pl.when(sec == 1)
        def _():
            node_in(m).wait()

        if m == 0:
            weights[0].wait()
            weights[1].wait()
        values = nl[m]
        rhs[:nodes] = dot(values, rhs[at_s:]).astype(BF16)
        rhs[at_r:at_s] = dot(values, w1r[...]).astype(BF16)

        for c in list(range(1, len(chunks))) + [0]:
            lo, hi = chunks[c]
            edge_in(m, c).wait()
            if m == 0 and c == 1:
                weights[2].wait()
                weights[3].wait()
            if c == 0:
                if m == 0:
                    @pl.when(sec == 0)
                    def _():
                        pltpu.make_async_copy(halo, halo, hsem.at[0]).wait()

                @pl.when(sec == 1)
                def _():
                    pltpu.make_async_copy(halo.at[:, m], halo.at[:, m], hsem.at[m]).wait()

                for p in range(peers):
                    hx[pl.ds(p * hcap, hcap)] = halo[p, m]
                from_far = dot(halo_hot, hx[...].astype(BF16)).astype(BF16)
                lat = el[m, lo:hi]
                lhs = jnp.concatenate([lat, ohr[lo:hi], from_far], axis=1)
                pre = dot(lhs, rhs[at_e:])
            else:
                lat = el[m, lo:hi]
                lhs = jnp.concatenate([ohs[lo:hi], lat, ohr[lo:hi]], axis=1)
                pre = dot(lhs, rhs[:at_s])
            hidden = silu(pre + bias_e).astype(BF16)
            update = layer_norm(dot(hidden, w2[...]), gain_e)
            slot = lax.broadcasted_iota(jnp.int32, (hi - lo, 1), 0) + lo
            update = update * (slot < live).astype(F32)
            msg[lo:hi] = update.astype(BF16)
            oel[m, lo:hi] = (lat.astype(F32) + update).astype(BF16)

            @pl.when(sec == 0)
            def _():
                edge_next(m, c).start()

            edge_res(m, c).start()

        if m == 0:
            for copy in weights[4:]:
                copy.wait()
        incoming = dot(ohrt[...], msg[...]).astype(BF16)
        values = nl[m]
        pre = dot(jnp.concatenate([values, incoming], axis=1), n1[...])
        hidden = silu(pre + bias_n).astype(BF16)
        update = layer_norm(dot(hidden, n2[...]), gain_n)
        onl[m] = (values.astype(F32) + update).astype(BF16)

        @pl.when(sec == 0)
        def _():
            node_next(m).start()

            def store(t, k, row):
                out1[m, t, pl.ds(k, 1)] = row

            gather_rows(onl[m], store)

            @pl.loop(0, peers)
            def _(step):
                target = peer(step)
                pltpu.make_async_remote_copy(
                    src_ref=out1.at[m, target], dst_ref=halo.at[me, m], send_sem=s1sem.at[m],
                    recv_sem=hsem.at[m], device_id={"section": 1, "dom": target},
                    device_id_type=pl.DeviceIdType.MESH).start()

        node_res(m).start()

    for m in range(batches):
        node_res(m).wait()
        for c in range(len(chunks)):
            edge_res(m, c).wait()

    @pl.when(sec == 0)
    def _():
        others = out0.at[pl.ds(0, peers - 1)]
        pltpu.make_async_copy(others, others, s0sem).wait()
        for m in range(batches):
            pltpu.make_async_copy(out1.at[m], out1.at[m], s1sem.at[m]).wait()
            node_next(m).wait_send()
            for c in range(len(chunks)):
                edge_next(m, c).wait_send()


def local(node_feats, edge_feats, edge_src, edge_dst, edge_count, send_rows,
          edge_w1, edge_b1, edge_w2, edge_gain, node_w1, node_b1, node_w2, node_gain):
    batches, nodes, width = node_feats.shape
    edges = edge_feats.shape[1]
    peers, hcap = send_rows.shape
    inner = edge_w2.shape[1]
    halo_rows = peers * hcap
    chunks = [(0, halo_rows)]
    while chunks[-1][1] < edges:
        start = chunks[-1][1]
        chunks.append((start, min(edges, (start // BLOCK + 1) * BLOCK)))
    slots = len(chunks) + 1
    anywhere = pl.BlockSpec(memory_space=pl.ANY)
    dma = pltpu.SemaphoreType.DMA
    flops = 2 * batches * width * inner * (3 * edges + 6 * nodes)
    moved = 2 * (2 * batches * (nodes + edges) * width + 7 * width * inner)
    return pl.pallas_call(
        functools.partial(kernel, peers, hcap, chunks),
        out_shape=(jax.ShapeDtypeStruct((1, batches, nodes, width), BF16),
                   jax.ShapeDtypeStruct((1, batches, edges, width), BF16)),
        in_specs=[anywhere] * 14,
        out_specs=(anywhere, anywhere),
        scratch_shapes=[
            pltpu.VMEM((1, 1), jnp.int32),
            pltpu.VMEM((1, edges), jnp.int32),
            pltpu.VMEM((1, edges), jnp.int32),
            pltpu.VMEM((hcap, peers), jnp.int32),
            pltpu.VMEM((1, inner), BF16),
            pltpu.VMEM((1, width), BF16),
            pltpu.VMEM((1, inner), BF16),
            pltpu.VMEM((1, width), BF16),
            pltpu.VMEM((batches, nodes, width), BF16),
            pltpu.VMEM((batches, edges, width), BF16),
            pltpu.VMEM((batches, nodes, width), BF16),
            pltpu.VMEM((batches, edges, width), BF16),
            pltpu.VMEM((2 * nodes + 2 * width, inner), BF16),
            pltpu.VMEM((width, inner), BF16),
            pltpu.VMEM((inner, width), BF16),
            pltpu.VMEM((2 * width, inner), BF16),
            pltpu.VMEM((inner, width), BF16),
            pltpu.VMEM((edges, width), BF16),
            pltpu.VMEM((edges, nodes), BF16),
            pltpu.VMEM((edges, nodes), BF16),
            pltpu.VMEM((nodes, edges), BF16),
            pltpu.VMEM((peers, batches, hcap, width), F32),
            pltpu.VMEM((batches, peers, hcap, width), F32),
            pltpu.VMEM((peers, batches, hcap, width), F32),
            pltpu.VMEM((halo_rows, width), F32),
            dma((15,)),
            dma((batches, slots)),
            dma((batches,)),
            dma((batches, slots)),
            dma,
            dma((batches,)),
            dma((batches, slots)),
        ],
        compiler_params=pltpu.CompilerParams(
            collective_id=0, has_side_effects=True, vmem_limit_bytes=64 * 1024 * 1024),
        cost_estimate=pl.CostEstimate(flops=flops, bytes_accessed=moved, transcendentals=0),
    )(edge_count.reshape(1, 1), edge_src.reshape(1, -1), edge_dst.reshape(1, -1), send_rows.T,
      edge_b1, edge_gain, node_b1, node_gain,
      node_feats, edge_feats, edge_w1, edge_w2, node_w1, node_w2)


def solution(mesh):
    in_specs = (
        P(None, "dom", None),
        P(None, "dom", None),
        P("dom"),
        P("dom"),
        P("dom"),
        P("dom", None),
        P("section", None, None, None),
        P("section", None),
        P("section", None, None),
        P("section", None),
        P("section", None, None, None),
        P("section", None),
        P("section", None, None),
        P("section", None),
    )
    out_specs = (P("section", None, "dom", None), P("section", None, "dom", None))
    return jax.shard_map(local, mesh=mesh, in_specs=in_specs, out_specs=out_specs, check_vma=False)
```
